256 devices in a mesh: group: 8 (over z), ep: 32 (over x, y, core).
Axes of the slice: x: 4, y: 4, z: 8, core: 2. Of those that a mesh axis runs over, the one named last changes fastest.
Arguments:
- tokens: bfloat16 [4096, 7168], P('ep', 'group'), may hold values from -6 to 6
- expert_ids: int32 [4096, 8], P('ep'), may hold values from 0 to 31, all different within a row; in each aligned block of 128 rows (0 to 127, 128 to 255, ...) at most 72 rows name the same one
- route_weights: float32 [4096, 8], P('ep'), may hold values from 0.1 to 1
- expert_slot: int32 [32], replicated, may hold values from 0 to 31, each once
- w_gate: bfloat16 [32, 7168, 1024], P('ep', 'group'), may hold values from -0.0625 to 0.0625
- w_up: bfloat16 [32, 7168, 1024], P('ep', 'group'), may hold values from -0.0625 to 0.0625
- w_down: bfloat16 [32, 1024, 7168], P('ep', None, 'group'), may hold values from -0.1875 to 0.1875
Outputs:
- mixed: bfloat16 [4096, 7168], P('ep', 'group')
The draws below stay inside these ranges and needn't reach their ends.
Inputs may be any that keep to these rules, and one draw needn't show every extreme that they name: `expert_ids`: each row names 8 different experts. Among the 128 rows of one index of ep (aligned blocks of rows), no expert is named by more than 72 rows, and in some block one expert is named by exactly 72. `expert_slot`: each index of ep holds exactly one expert.
All inputs are finite; a program needn't handle non-finite values.
Results may differ from the reference program's by a relative error of at most 0.029.
Values may be sent and summed in bfloat16 or wider, within the bound.
No kernel may reach another device: no remote copies, remote signals or barrier semaphores. Data moves between devices by JAX's collectives and lax.ppermute only.
A program may use at most 64 MiB of HBM per device.

```python
import math
import jax
import jax.numpy as jnp
import numpy as np
from jax import lax

D = 7168
FF = 1024
TOPK = 8
TOK_EP = 128
EXPERTS = 32
TOKENS = 4096
CAP = 72
N_GROUP = 8
N_EP = 32


def levels(own_key, extent, pieces, least, top_value):
    level, own = 1.0, jax.random.fold_in(own_key, 6)
    for dim, blocks in pieces:
        draws = jnp.exp(jax.random.uniform(jax.random.fold_in(own, dim), (blocks,), jnp.float32, least / len(pieces), top_value / len(pieces)))
        level = level * jnp.repeat(draws, extent[dim] // blocks).reshape([-1 if axis == dim else 1 for axis in range(len(extent))])
    return level


def deal_out(key, own, number, rows, number_of, top, limit, slope):
    sequence = jax.random.permutation(key, number_of)
    crowded, usual = portions_of(number_of, rows * top, limit, slope, True), portions_of(number_of, rows * top, limit, slope, False)
    places = jnp.arange(number_of)

    def named(lengths, offset_by):
        used = int((lengths > 0).sum())
        fixed = max(1, used // 4)
        moved = fixed + (places - fixed + offset_by * (used - fixed)) % max(1, number_of - fixed)
        return jnp.zeros((number_of,), jnp.int32).at[sequence[jnp.where(places < fixed, places, moved)]].set(jnp.asarray(lengths, jnp.int32))

    lengths = jnp.where(number % 4 == 0, named(crowded, number // 4), named(usual, number - number // 4 - 1))
    mixed = jax.random.permutation(jax.random.fold_in(own, 3), number_of)
    donor, taker = mixed[0:number_of // 2 * 2:2], mixed[1:number_of // 2 * 2:2]
    margin = jnp.minimum(lengths[donor] - 1, limit - lengths[taker]) // 2
    margin = jnp.where((donor == sequence[0]) | (taker == sequence[0]) | (lengths[taker] == 0), 0, jnp.maximum(margin, 0))
    moved = jax.random.randint(jax.random.fold_in(own, 4), (number_of // 2,), 0, 1 << 20) % (margin + 1)
    lengths = lengths.at[donor].add(-moved).at[taker].add(moved)
    labels = jnp.searchsorted(jnp.cumsum(lengths), jnp.arange(rows * top), side="right").astype(jnp.int32)
    grid = labels.reshape(top, rows).T
    grid = grid[jax.random.permutation(jax.random.fold_in(own, 1), rows)]
    offset_by = jax.random.randint(jax.random.fold_in(own, 2), (rows, 1), 0, top)
    return jnp.take_along_axis(grid, (jnp.arange(top)[None, :] + offset_by) % top, axis=1)


def portions_of(amount, total, reach, lean, full):
    portions = [(1 << 20) // math.isqrt(standing ** lean) + 1 for standing in range(1, amount + 1)]
    largest = reach if full else min(reach, max(-(-total // amount), total * portions[0] // sum(portions)))
    least = 1 if total - largest >= amount - 1 else 0
    counts, rest = [largest] + [least] * (amount - 1), total - largest - least * (amount - 1)
    while rest > 0:
        candidates = [i for i in range(1, amount) if counts[i] < largest] or [i for i in range(1, amount) if counts[i] < reach]
        pool, left = sum([portions[i] for i in candidates]), rest
        for i in candidates:
            more = min(reach - counts[i], max(1, left * portions[i] // pool), rest)
            counts[i] = counts[i] + more
            rest = rest - more
    return np.array(counts)


def noise(key, shape, scale, most, cuts=(), kind=jnp.bfloat16):
    loudness = levels(key, shape, cuts, -0.22, 0.18) if cuts else 1.0
    values = jax.random.normal(key, shape, jnp.float32) * scale * loudness
    return jnp.minimum(jnp.maximum(values, -most), most).astype(kind)


def setup_inputs(seed: int = 0) -> dict:
    seeds = jax.random.split(jax.random.key(seed), 8)
    tokens = noise(seeds[0], (TOKENS, D), 1.0, 6.0, ((0, 32), (1, 8)))
    expert_ids_keys = jax.random.split(jax.random.fold_in(seeds[1], 1), TOKENS // TOK_EP)
    expert_ids_turns = jax.random.permutation(jax.random.fold_in(seeds[1], 3), TOKENS // TOK_EP)
    expert_ids = jax.vmap(lambda own, number: deal_out(jax.random.fold_in(seeds[1], 2), own, number, TOK_EP, EXPERTS, TOPK, CAP, 2))(expert_ids_keys, expert_ids_turns).reshape((TOKENS, TOPK))
    route_weights = jnp.clip(0.1 + 0.9 * jax.random.uniform(seeds[2], (TOKENS, TOPK), jnp.float32) ** levels(seeds[2], (TOKENS, TOPK), ((0, 32),), -0.2, 0.2), 0.1, 1.0)
    expert_slot = jax.random.permutation(seeds[3], EXPERTS).astype(jnp.int32)
    w_gate = noise(seeds[4], (EXPERTS, D, FF), D ** -0.5, 0.0625, ((0, 32), (1, 8)))
    w_up = noise(seeds[5], (EXPERTS, D, FF), D ** -0.5, 0.0625, ((0, 32), (1, 8)))
    w_down = noise(seeds[6], (EXPERTS, FF, D), FF ** -0.5, 0.1875, ((0, 32), (2, 8)))
    return {"tokens": tokens, "expert_ids": expert_ids, "route_weights": route_weights, "expert_slot": expert_slot, "w_gate": w_gate, "w_up": w_up, "w_down": w_down}


def split_sum(rows, weight):
    grouped_rows = rows.reshape(rows.shape[0], N_GROUP, D // N_GROUP).astype(jnp.float32)
    grouped_weight = weight.reshape(N_GROUP, D // N_GROUP, FF).astype(jnp.float32)
    partial_value = jnp.einsum("rgd,gdf->rgf", grouped_rows, grouped_weight)
    rounded = lax.optimization_barrier(partial_value.astype(jnp.bfloat16))
    return jnp.sum(rounded.astype(jnp.float32), axis=1)


def reference(tokens, expert_ids, route_weights, expert_slot, w_gate, w_up, w_down):
    pair_slot = jnp.take(expert_slot, expert_ids.reshape(-1)).astype(jnp.int32)
    pair_token = (jnp.arange(TOKENS * TOPK, dtype=jnp.int32) // TOPK).astype(jnp.int32)
    pair_weight = route_weights.reshape(-1).astype(jnp.float32)
    buffer_rows = N_EP * CAP
    padded = jnp.concatenate([tokens, jnp.zeros((1, D), tokens.dtype)], axis=0)

    def per_slot(running, slot_index):
        chosen = pair_slot == slot_index
        position = jnp.cumsum(chosen.astype(jnp.int32)) - 1
        target = jnp.where(chosen, position, buffer_rows).astype(jnp.int32)
        row_table = jnp.full((buffer_rows + 1,), TOKENS, jnp.int32).at[target].set(pair_token)[:buffer_rows]
        weight_table = jnp.zeros((buffer_rows + 1,), jnp.float32).at[target].set(pair_weight)[:buffer_rows]
        gathered = padded[row_table]
        gate = split_sum(gathered, w_gate[slot_index])
        up = split_sum(gathered, w_up[slot_index])
        hidden = (jax.nn.silu(gate) * up).astype(jnp.bfloat16)
        expert_out = jnp.dot(hidden, w_down[slot_index], preferred_element_type=jnp.float32).astype(jnp.bfloat16)
        running = running.at[row_table].add(expert_out.astype(jnp.float32) * weight_table[:, None])
        return running, jnp.zeros((), jnp.float32)

    running = jnp.zeros((TOKENS + 1, D), jnp.float32)
    running, ignored = lax.scan(per_slot, running, jnp.arange(N_EP, dtype=jnp.int32))
    return running[:TOKENS].astype(jnp.bfloat16)
```

```python
import jax
import jax.numpy as jnp
from jax import lax
from jax.sharding import PartitionSpec as P

N_Z = 8
N_X = 4
N_Y = 4
CAP = 72
META_ROWS = 16
BF = jnp.bfloat16
F32 = jnp.float32


def hop(value, dz=0, dx=0, dy=0, mirror=False, swap=False):
    pairs = []
    for z in range(N_Z):
        for x in range(N_X):
            for y in range(N_Y):
                for c in range(2):
                    sign = -1 if (mirror and c) else 1
                    to_z = (z + sign * dz) % N_Z
                    to_x = (x + sign * dx) % N_X
                    to_y = (y + sign * dy) % N_Y
                    to_c = 1 - c if swap else c
                    here = ((z * N_X + x) * N_Y + y) * 2 + c
                    there = ((to_z * N_X + to_x) * N_Y + to_y) * 2 + to_c
                    pairs.append((here, there))
    return lax.ppermute(value, ("group", "ep"), pairs)


def add(first, second):
    return (first.astype(F32) + second.astype(F32)).astype(BF)


def pack(tokens, expert_ids, route_weights):
    high = route_weights.astype(BF)
    low = (route_weights - high.astype(F32)).astype(BF)
    ids = expert_ids.astype(BF)
    left = jnp.concatenate([ids.T, high.T], axis=0)
    right = jnp.concatenate([low.T, jnp.zeros_like(low.T)], axis=0)
    meta = jnp.concatenate([left, right], axis=1)
    meta = jnp.pad(meta, ((0, 0), (0, tokens.shape[1] - meta.shape[1])))
    return jnp.concatenate([tokens, meta], axis=0)


def selection(blocks, own_expert):
    rows = blocks.shape[1] - META_ROWS
    meta = blocks[:, rows:, :]
    ids = meta[:, 0:8, 0:rows]
    high = meta[:, 8:16, 0:rows].astype(F32)
    low = meta[:, 0:8, rows:2 * rows].astype(F32)
    hot = ids == own_expert.astype(BF)
    chosen = jnp.any(hot, axis=1)
    weight = jnp.sum(jnp.where(hot, high + low, 0.0), axis=1)
    order = jnp.arange(rows)
    before = (order[:, None] < order[None, :]).astype(BF)
    position = jnp.dot(chosen.astype(BF), before, preferred_element_type=F32).astype(jnp.int32)
    spot = jnp.where(chosen, position, -1)
    one_hot = (spot[:, None, :] == jnp.arange(CAP)[None, :, None]).astype(BF)
    return one_hot, weight


def turn(value, start):
    return lax.dynamic_slice_in_dim(jnp.concatenate([value, value], axis=0), start, N_Z, axis=0)


def z_phase(rows, w_gate_up, w_down):
    count, cap, width = rows.shape
    part = jnp.dot(
        rows.reshape(count * cap, width), w_gate_up, preferred_element_type=F32
    ).astype(BF).reshape(count, cap, w_gate_up.shape[1])
    ahead = hop(part[4], dz=1, mirror=True)
    back = hop(part[5], dz=-1, mirror=True)
    ahead = hop(add(ahead, part[3]), dz=1, mirror=True)
    back = hop(add(back, part[6]), dz=-1, mirror=True)
    ahead = hop(add(ahead, part[2]), dz=1, mirror=True)
    back = hop(add(back, part[7]), dz=-1, mirror=True)
    ahead = hop(add(ahead, part[1]), dz=1, mirror=True)
    total = part[0].astype(F32) + ahead.astype(F32) + back.astype(F32)
    hidden_width = w_gate_up.shape[1] // 2
    gate, up = total[:, :hidden_width], total[:, hidden_width:]
    own = (jax.nn.silu(gate) * up).astype(BF)
    seventh = hop(own, dz=1, mirror=True)
    first = hop(own, dz=-1, mirror=True)
    sixth = hop(seventh, dz=1, mirror=True)
    second = hop(first, dz=-1, mirror=True)
    fifth = hop(sixth, dz=1, mirror=True)
    third = hop(second, dz=-1, mirror=True)
    fourth = hop(fifth, dz=1, mirror=True)
    hidden = jnp.concatenate(
        [own, first, second, third, fourth, fifth, sixth, seventh], axis=0
    )
    out = jnp.dot(hidden, w_down, preferred_element_type=F32).astype(BF)
    return out.reshape(count, cap, w_down.shape[1])


def per_device(tokens, expert_ids, route_weights, expert_slot, w_gate, w_up, w_down):
    z = lax.axis_index("group")
    ep = lax.axis_index("ep")
    core = ep % 2
    own_expert = jnp.sum(jnp.where(expert_slot == ep, jnp.arange(expert_slot.shape[0]), 0))
    start = jnp.where(core == 0, z, (N_Z - z) % N_Z)
    finish = (N_Z - start) % N_Z
    w_gate_up = jnp.concatenate([w_gate[0], w_up[0]], axis=1)
    block = pack(tokens, expert_ids, route_weights)
    from_behind = hop(block, dy=1, mirror=True)
    from_ahead = hop(block, dy=-1, mirror=True)
    opposite = hop(from_behind, dy=1, mirror=True)
    column = jnp.stack([block, from_ahead, opposite, from_behind])
    columns = [column, None, None, None]
    columns[3] = hop(column, dx=1)
    columns[1] = hop(column, dx=-1)
    columns[2] = hop(columns[3], dx=1)
    results = []
    for index in (0, 1, 2, 3):
        with jax.named_scope("chunk" + str(index)):
            mate = hop(columns[index], swap=True)
            blocks = jnp.concatenate([columns[index], mate], axis=0)
            one_hot, weight = selection(blocks, own_expert)
            token_rows = blocks[:, : tokens.shape[0]]
            rows = jnp.einsum(
                "bjt,btd->bjd", one_hot, token_rows, preferred_element_type=F32
            ).astype(BF)
            out = turn(z_phase(turn(rows, start), w_gate_up, w_down[0]), finish)
            dense = jnp.einsum("bjt,bjd->btd", one_hot, out, preferred_element_type=F32)
            dense = (dense * weight[:, :, None]).astype(BF)
            half = dense.shape[0] // 2
            kept = add(dense[:half], hop(dense[half:], swap=True))
            relayed = hop(kept[2], dy=1, mirror=True)
            to_next = hop(add(kept[1], relayed), dy=1, mirror=True)
            to_last = hop(kept[3], dy=-1, mirror=True)
            results.append(
                kept[0].astype(F32) + to_next.astype(F32) + to_last.astype(F32)
            )
    relayed = hop(results[2].astype(BF), dx=1)
    to_next = hop((results[1] + relayed.astype(F32)).astype(BF), dx=1)
    to_last = hop(results[3].astype(BF), dx=-1)
    return (results[0] + to_next.astype(F32) + to_last.astype(F32)).astype(BF)


def solution(mesh):
    in_specs = (
        P("ep", "group"),
        P("ep", None),
        P("ep", None),
        P(),
        P("ep", "group", None),
        P("ep", "group", None),
        P("ep", None, "group"),
    )
    out_specs = P("ep", "group")
    return jax.shard_map(
        per_device, mesh=mesh, in_specs=in_specs, out_specs=out_specs, check_vma=False
    )
```

```python
import jax
import jax.numpy as jnp
from jax import lax
from jax.sharding import PartitionSpec as P

N_Z = 8
N_X = 4
N_Y = 4
CAP = 72
META_ROWS = 16
BF = jnp.bfloat16
F32 = jnp.float32


def hop(value, dz=0, dx=0, dy=0, mirror=False, swap=False):
    pairs = []
    for z in range(N_Z):
        for x in range(N_X):
            for y in range(N_Y):
                for c in range(2):
                    sign = -1 if (mirror and c) else 1
                    to_z = (z + sign * dz) % N_Z
                    to_x = (x + sign * dx) % N_X
                    to_y = (y + sign * dy) % N_Y
                    to_c = 1 - c if swap else c
                    here = ((z * N_X + x) * N_Y + y) * 2 + c
                    there = ((to_z * N_X + to_x) * N_Y + to_y) * 2 + to_c
                    pairs.append((here, there))
    return lax.ppermute(value, ("group", "ep"), pairs)


def add(first, second):
    return (first.astype(F32) + second.astype(F32)).astype(BF)


def pack(tokens, expert_ids, route_weights):
    high = route_weights.astype(BF)
    low = (route_weights - high.astype(F32)).astype(BF)
    ids = expert_ids.astype(BF)
    left = jnp.concatenate([ids.T, high.T], axis=0)
    right = jnp.concatenate([low.T, jnp.zeros_like(low.T)], axis=0)
    meta = jnp.concatenate([left, right], axis=1)
    meta = jnp.pad(meta, ((0, 0), (0, tokens.shape[1] - meta.shape[1])))
    return jnp.concatenate([tokens, meta], axis=0)


def selection(blocks, own_expert):
    rows = blocks.shape[1] - META_ROWS
    meta = blocks[:, rows:, :]
    ids = meta[:, 0:8, 0:rows]
    high = meta[:, 8:16, 0:rows].astype(F32)
    low = meta[:, 0:8, rows:2 * rows].astype(F32)
    hot = ids == own_expert.astype(BF)
    chosen = jnp.any(hot, axis=1)
    weight = jnp.sum(jnp.where(hot, high + low, 0.0), axis=1)
    order = jnp.arange(rows)
    before = (order[:, None] < order[None, :]).astype(BF)
    position = jnp.dot(chosen.astype(BF), before, preferred_element_type=F32).astype(jnp.int32)
    spot = jnp.where(chosen, position, -1)
    one_hot = (spot[:, None, :] == jnp.arange(CAP)[None, :, None]).astype(BF)
    return one_hot, weight


def turn(value, start):
    return lax.dynamic_slice_in_dim(jnp.concatenate([value, value], axis=0), start, N_Z, axis=0)


def ring_sum(part):
    ahead = hop(part[4], dz=1, mirror=True)
    back = hop(part[5], dz=-1, mirror=True)
    ahead = hop(add(ahead, part[3]), dz=1, mirror=True)
    back = hop(add(back, part[6]), dz=-1, mirror=True)
    ahead = hop(add(ahead, part[2]), dz=1, mirror=True)
    back = hop(add(back, part[7]), dz=-1, mirror=True)
    ahead = hop(add(ahead, part[1]), dz=1, mirror=True)
    total = part[0].astype(F32) + ahead.astype(F32) + back.astype(F32)
    hidden_width = part.shape[-1] // 2
    gate_sum, up_sum = total[:, :hidden_width], total[:, hidden_width:]
    return (jax.nn.silu(gate_sum) * up_sum).astype(BF)


def ring_gather(own):
    behind, front = [own], [own]
    for step in range(1, 5):
        behind.append(hop(behind[-1], dz=1, mirror=True))
        if step < 4:
            front.append(hop(front[-1], dz=-1, mirror=True))
    return front + behind[:0:-1]


def pick_rows(column, mate, own_expert, row_count):
    blocks = jnp.concatenate([column, mate], axis=0)
    one_hot, weight = selection(blocks, own_expert)
    rows = jnp.einsum(
        "bjt,btd->bjd", one_hot, blocks[:, :row_count], preferred_element_type=F32
    ).astype(BF)
    return rows, one_hot, weight


def spread(one_hot, weight, out):
    dense = jnp.einsum("bjt,bjd->btd", one_hot, out, preferred_element_type=F32)
    return (dense * weight[:, :, None]).astype(BF)


def core_and_y_sum(dense):
    half = dense.shape[0] // 2
    kept = add(dense[:half], hop(dense[half:], swap=True))
    to_next = hop(kept[1], dy=1, mirror=True)
    to_last = hop(kept[3], dy=-1, mirror=True)
    across = hop(kept[2], dy=2, mirror=True)
    return (
        kept[0].astype(F32) + to_next.astype(F32)
        + to_last.astype(F32) + across.astype(F32)
    )


def per_device(tokens, expert_ids, route_weights, expert_slot, w_gate, w_up, w_down):
    z = lax.axis_index("group")
    ep = lax.axis_index("ep")
    core = ep % 2
    row_count = tokens.shape[0]
    own_expert = jnp.sum(jnp.where(expert_slot == ep, jnp.arange(expert_slot.shape[0]), 0))
    start = jnp.where(core == 0, z, (N_Z - z) % N_Z)
    w_gate_up = jnp.concatenate([w_gate[0], w_up[0]], axis=1)
    down = w_down[0]
    block = pack(tokens, expert_ids, route_weights)
    from_behind = hop(block, dy=1, mirror=True)
    from_ahead = hop(block, dy=-1, mirror=True)
    from_below = hop(block, dx=1)
    from_above = hop(block, dx=-1)
    opposite = hop(block, dy=2, mirror=True)
    sides = jnp.stack([from_above, from_below])
    sides_behind = hop(sides, dy=1, mirror=True)
    sides_ahead = hop(sides, dy=-1, mirror=True)
    opposite_above = hop(opposite, dx=-1)
    opposite_below = hop(opposite, dx=1)
    column = jnp.stack([block, from_ahead, opposite, from_behind])
    mate = hop(column, swap=True)

    def prepared(column, mate):
        rows, one_hot, weight = pick_rows(column, mate, own_expert, row_count)
        rows = turn(rows, start)
        part = jnp.dot(
            rows.reshape(-1, rows.shape[-1]), w_gate_up, preferred_element_type=F32
        )
        part = part.astype(BF).reshape(rows.shape[:2] + (w_gate_up.shape[1],))
        return part, one_hot, weight

    def combined(first, second, hidden):
        out = jnp.zeros((N_Z,) + hidden[0].shape[:2] + (down.shape[1],), BF)
        for k, value in enumerate(hidden):
            flat = value.reshape(-1, value.shape[-1])
            piece = jnp.dot(flat, down, preferred_element_type=F32).astype(BF)
            piece = piece.reshape((1,) + value.shape[:2] + (down.shape[1],))
            out = lax.dynamic_update_slice(out, piece, ((start + k) % N_Z, 0, 0, 0))
        dense = jnp.stack(
            [spread(first[1], first[2], out[:, 0]), spread(second[1], second[2], out[:, 1])],
            axis=1,
        )
        return core_and_y_sum(dense)

    chunk_0 = prepared(column, mate)
    above = jnp.stack([from_above, sides_ahead[0], opposite_above, sides_behind[0]])
    below = jnp.stack([from_below, sides_ahead[1], opposite_below, sides_behind[1]])
    far = hop(jnp.where(core == 0, below, above), dx=1, mirror=True)
    chunk_1 = prepared(above, hop(above, swap=True))
    hidden_0 = ring_sum(chunk_0[0])
    chunk_3 = prepared(below, hop(below, swap=True))
    hidden_1 = ring_sum(chunk_1[0])
    chunk_2 = prepared(far, hop(far, swap=True))
    hidden_3 = ring_sum(chunk_3[0])
    hidden_2 = ring_sum(chunk_2[0])
    gathered = ring_gather(jnp.stack([hidden_0, hidden_1]))
    result_01 = combined(chunk_0, chunk_1, gathered)
    to_next = hop(result_01[1].astype(BF), dx=1)
    gathered = ring_gather(jnp.stack([hidden_2, hidden_3]))
    result_23 = combined(chunk_2, chunk_3, gathered)
    across = hop(result_23[0].astype(BF), dx=2)
    to_last = hop(result_23[1].astype(BF), dx=-1)
    return (
        result_01[0] + to_next.astype(F32) + to_last.astype(F32) + across.astype(F32)
    ).astype(BF)


def solution(mesh):
    in_specs = (
        P("ep", "group"),
        P("ep", None),
        P("ep", None),
        P(),
        P("ep", "group", None),
        P("ep", "group", None),
        P("ep", None, "group"),
    )
    out_specs = P("ep", "group")
    return jax.shard_map(
        per_device, mesh=mesh, in_specs=in_specs, out_specs=out_specs, check_vma=False
    )
```

```python
import jax
import jax.numpy as jnp
from jax import lax
from jax.sharding import PartitionSpec as P

N_Z = 8
N_X = 4
N_Y = 4
CAP = 72
META_ROWS = 16
BF = jnp.bfloat16
F32 = jnp.float32


def hop(value, dz=0, dx=0, dy=0, mirror=False, swap=False):
    pairs = []
    for z in range(N_Z):
        for x in range(N_X):
            for y in range(N_Y):
                for c in range(2):
                    sign = -1 if (mirror and c) else 1
                    to_z = (z + sign * dz) % N_Z
                    to_x = (x + sign * dx) % N_X
                    to_y = (y + sign * dy) % N_Y
                    to_c = 1 - c if swap else c
                    here = ((z * N_X + x) * N_Y + y) * 2 + c
                    there = ((to_z * N_X + to_x) * N_Y + to_y) * 2 + to_c
                    pairs.append((here, there))
    return lax.ppermute(value, ("group", "ep"), pairs)


def crossing(value, step, stage):
    pairs = []
    for z in range(N_Z):
        for x in range(N_X):
            for y in range(N_Y):
                for c in range(2):
                    to_x, to_y = x, y
                    if stage == c:
                        to_y = (y + (1 - 2 * c) * step) % N_Y
                    else:
                        to_x = (x + step) % N_X
                    here = ((z * N_X + x) * N_Y + y) * 2 + c
                    there = ((z * N_X + to_x) * N_Y + to_y) * 2 + c
                    pairs.append((here, there))
    return lax.ppermute(value, ("group", "ep"), pairs)


def crossing_sum(groups, stage):
    to_next = crossing(groups[1], 1, stage)
    to_last = crossing(groups[3], -1, stage)
    across = crossing(groups[2], 2, stage)
    return (
        groups[0].astype(F32) + to_next.astype(F32)
        + to_last.astype(F32) + across.astype(F32)
    )


def add(first, second):
    return (first.astype(F32) + second.astype(F32)).astype(BF)


def pack(tokens, expert_ids, route_weights):
    high = route_weights.astype(BF)
    low = (route_weights - high.astype(F32)).astype(BF)
    ids = expert_ids.astype(BF)
    left = jnp.concatenate([ids.T, high.T], axis=0)
    right = jnp.concatenate([low.T, jnp.zeros_like(low.T)], axis=0)
    meta = jnp.concatenate([left, right], axis=1)
    meta = jnp.pad(meta, ((0, 0), (0, tokens.shape[1] - meta.shape[1])))
    return jnp.concatenate([tokens, meta], axis=0)


def selection(blocks, own_expert):
    rows = blocks.shape[1] - META_ROWS
    meta = blocks[:, rows:, :]
    ids = meta[:, 0:8, 0:rows]
    high = meta[:, 8:16, 0:rows].astype(F32)
    low = meta[:, 0:8, rows:2 * rows].astype(F32)
    hot = ids == own_expert.astype(BF)
    chosen = jnp.any(hot, axis=1)
    weight = jnp.sum(jnp.where(hot, high + low, 0.0), axis=1)
    order = jnp.arange(rows)
    before = (order[:, None] < order[None, :]).astype(BF)
    position = jnp.dot(chosen.astype(BF), before, preferred_element_type=F32).astype(jnp.int32)
    spot = jnp.where(chosen, position, -1)
    one_hot = (spot[:, None, :] == jnp.arange(CAP)[None, :, None]).astype(BF)
    return one_hot, weight


def turn(value, start):
    return lax.dynamic_slice_in_dim(jnp.concatenate([value, value], axis=0), start, N_Z, axis=0)


def ring_sum(part):
    ahead = hop(part[4], dz=1, mirror=True)
    back = hop(part[5], dz=-1, mirror=True)
    ahead = hop(add(ahead, part[3]), dz=1, mirror=True)
    back = hop(add(back, part[6]), dz=-1, mirror=True)
    ahead = hop(add(ahead, part[2]), dz=1, mirror=True)
    back = hop(add(back, part[7]), dz=-1, mirror=True)
    ahead = hop(add(ahead, part[1]), dz=1, mirror=True)
    total = part[0].astype(F32) + ahead.astype(F32) + back.astype(F32)
    hidden_width = part.shape[-1] // 2
    gate_sum, up_sum = total[:, :hidden_width], total[:, hidden_width:]
    return (jax.nn.silu(gate_sum) * up_sum).astype(BF)


def ring_gather(own):
    behind, front = [own], [own]
    for step in range(1, 5):
        behind.append(hop(behind[-1], dz=1, mirror=True))
        if step < 4:
            front.append(hop(front[-1], dz=-1, mirror=True))
    return front + behind[:0:-1]


def pick_rows(column, mate, own_expert, row_count):
    blocks = jnp.concatenate([column, mate], axis=0)
    one_hot, weight = selection(blocks, own_expert)
    rows = jnp.einsum(
        "bjt,btd->bjd", one_hot, blocks[:, :row_count], preferred_element_type=F32
    ).astype(BF)
    return rows, one_hot, weight


def spread(one_hot, weight, out):
    dense = jnp.einsum("bjt,bjd->btd", one_hot, out, preferred_element_type=F32)
    return (dense * weight[:, :, None]).astype(BF)


def core_sum(dense):
    half = dense.shape[0] // 2
    return add(dense[:half], hop(dense[half:], swap=True))


def per_device(tokens, expert_ids, route_weights, expert_slot, w_gate, w_up, w_down):
    z = lax.axis_index("group")
    ep = lax.axis_index("ep")
    core = ep % 2
    row_count = tokens.shape[0]
    own_expert = jnp.sum(jnp.where(expert_slot == ep, jnp.arange(expert_slot.shape[0]), 0))
    start = jnp.where(core == 0, z, (N_Z - z) % N_Z)
    w_gate_up = jnp.concatenate([w_gate[0], w_up[0]], axis=1)
    down = w_down[0]
    block = pack(tokens, expert_ids, route_weights)
    from_behind = hop(block, dy=1, mirror=True)
    from_ahead = hop(block, dy=-1, mirror=True)
    from_below = hop(block, dx=1)
    from_above = hop(block, dx=-1)
    opposite = hop(block, dy=2, mirror=True)
    sides = jnp.stack([from_above, from_below])
    sides_behind = hop(sides, dy=1, mirror=True)
    sides_ahead = hop(sides, dy=-1, mirror=True)
    opposite_above = hop(opposite, dx=-1)
    opposite_below = hop(opposite, dx=1)
    column = jnp.stack([block, from_ahead, opposite, from_behind])
    mate = hop(column, swap=True)

    def prepared(column, mate):
        rows, one_hot, weight = pick_rows(column, mate, own_expert, row_count)
        rows = turn(rows, start)
        part = jnp.dot(
            rows.reshape(-1, rows.shape[-1]), w_gate_up, preferred_element_type=F32
        )
        part = part.astype(BF).reshape(rows.shape[:2] + (w_gate_up.shape[1],))
        return part, one_hot, weight

    def combined(first, second, hidden):
        out = jnp.zeros((N_Z,) + hidden[0].shape[:2] + (down.shape[1],), BF)
        for k, value in enumerate(hidden):
            flat = value.reshape(-1, value.shape[-1])
            piece = jnp.dot(flat, down, preferred_element_type=F32).astype(BF)
            piece = piece.reshape((1,) + value.shape[:2] + (down.shape[1],))
            out = lax.dynamic_update_slice(out, piece, ((start + k) % N_Z, 0, 0, 0))
        dense = jnp.stack(
            [spread(first[1], first[2], out[:, 0]), spread(second[1], second[2], out[:, 1])],
            axis=1,
        )
        return core_sum(dense)

    chunk_0 = prepared(column, mate)
    above = jnp.stack([from_above, sides_ahead[0], opposite_above, sides_behind[0]])
    below = jnp.stack([from_below, sides_ahead[1], opposite_below, sides_behind[1]])
    far = hop(jnp.where(core == 0, below, above), dx=1, mirror=True)
    chunk_1 = prepared(above, hop(above, swap=True))
    hidden_0 = ring_sum(chunk_0[0])
    chunk_3 = prepared(below, hop(below, swap=True))
    hidden_1 = ring_sum(chunk_1[0])
    chunk_2 = prepared(far, hop(far, swap=True))
    hidden_3 = ring_sum(chunk_3[0])
    hidden_2 = ring_sum(chunk_2[0])
    gathered = ring_gather(jnp.stack([hidden_0, hidden_1]))
    kept_01 = combined(chunk_0, chunk_1, gathered)
    gathered = ring_gather(jnp.stack([hidden_2, hidden_3]))
    kept_23 = combined(chunk_2, chunk_3, gathered)
    kept = jnp.concatenate([kept_01, kept_23], axis=1)
    kept = jnp.where(core == 0, kept, jnp.swapaxes(kept, 0, 1))
    partly = crossing_sum(kept, 0).astype(BF)
    return crossing_sum(partly, 1).astype(BF)


def solution(mesh):
    in_specs = (
        P("ep", "group"),
        P("ep", None),
        P("ep", None),
        P(),
        P("ep", "group", None),
        P("ep", "group", None),
        P("ep", None, "group"),
    )
    out_specs = P("ep", "group")
    return jax.shard_map(
        per_device, mesh=mesh, in_specs=in_specs, out_specs=out_specs, check_vma=False
    )
```

```python
import jax
import jax.numpy as jnp
from jax import lax
from jax.sharding import PartitionSpec as P

N_Z = 8
N_X = 4
N_Y = 4
CAP = 72
META_ROWS = 16
BF = jnp.bfloat16
F32 = jnp.float32


def hop(value, dz=0, dx=0, dy=0, mirror=False, swap=False):
    pairs = []
    for z in range(N_Z):
        for x in range(N_X):
            for y in range(N_Y):
                for c in range(2):
                    sign = -1 if (mirror and c) else 1
                    to_z = (z + sign * dz) % N_Z
                    to_x = (x + sign * dx) % N_X
                    to_y = (y + sign * dy) % N_Y
                    to_c = 1 - c if swap else c
                    here = ((z * N_X + x) * N_Y + y) * 2 + c
                    there = ((to_z * N_X + to_x) * N_Y + to_y) * 2 + to_c
                    pairs.append((here, there))
    return lax.ppermute(value, ("group", "ep"), pairs)


def crossing(value, step, stage):
    pairs = []
    for z in range(N_Z):
        for x in range(N_X):
            for y in range(N_Y):
                for c in range(2):
                    to_x, to_y = x, y
                    if stage == c:
                        to_y = (y + (1 - 2 * c) * step) % N_Y
                    else:
                        to_x = (x + step) % N_X
                    here = ((z * N_X + x) * N_Y + y) * 2 + c
                    there = ((z * N_X + to_x) * N_Y + to_y) * 2 + c
                    pairs.append((here, there))
    return lax.ppermute(value, ("group", "ep"), pairs)


def crossing_sum(groups, stage):
    to_next = crossing(groups[1], 1, stage)
    to_last = crossing(groups[3], -1, stage)
    across = crossing(groups[2], 2, stage)
    return (
        groups[0].astype(F32) + to_next.astype(F32)
        + to_last.astype(F32) + across.astype(F32)
    )


def add(first, second):
    return (first.astype(F32) + second.astype(F32)).astype(BF)


def pack(tokens, expert_ids, route_weights):
    high = route_weights.astype(BF)
    low = (route_weights - high.astype(F32)).astype(BF)
    ids = expert_ids.astype(BF)
    left = jnp.concatenate([ids.T, high.T], axis=0)
    right = jnp.concatenate([low.T, jnp.zeros_like(low.T)], axis=0)
    meta = jnp.concatenate([left, right], axis=1)
    meta = jnp.pad(meta, ((0, 0), (0, tokens.shape[1] - meta.shape[1])))
    return jnp.concatenate([tokens, meta], axis=0)


def selection(blocks, own_expert):
    rows = blocks.shape[1] - META_ROWS
    meta = blocks[:, rows:, :]
    ids = meta[:, 0:8, 0:rows]
    high = meta[:, 8:16, 0:rows].astype(F32)
    low = meta[:, 0:8, rows:2 * rows].astype(F32)
    hot = ids == own_expert.astype(BF)
    chosen = jnp.any(hot, axis=1)
    weight = jnp.sum(jnp.where(hot, high + low, 0.0), axis=1)
    order = jnp.arange(rows)
    before = (order[:, None] < order[None, :]).astype(BF)
    position = jnp.dot(chosen.astype(BF), before, preferred_element_type=F32).astype(jnp.int32)
    spot = jnp.where(chosen, position, -1)
    one_hot = (spot[:, None, :] == jnp.arange(CAP)[None, :, None]).astype(BF)
    return one_hot, weight


def turn(value, start):
    return lax.dynamic_slice_in_dim(jnp.concatenate([value, value], axis=0), start, N_Z, axis=0)


def ring_sum(part):
    ahead = hop(part[4], dz=1, mirror=True)
    back = hop(part[5], dz=-1, mirror=True)
    ahead = hop(add(ahead, part[3]), dz=1, mirror=True)
    back = hop(add(back, part[6]), dz=-1, mirror=True)
    ahead = hop(add(ahead, part[2]), dz=1, mirror=True)
    back = hop(add(back, part[7]), dz=-1, mirror=True)
    ahead = hop(add(ahead, part[1]), dz=1, mirror=True)
    total = part[0].astype(F32) + ahead.astype(F32) + back.astype(F32)
    hidden_width = part.shape[-1] // 2
    gate_sum, up_sum = total[:, :hidden_width], total[:, hidden_width:]
    return (jax.nn.silu(gate_sum) * up_sum).astype(BF)


def ring_gather(own):
    behind, front = [own], [own]
    for step in range(1, 5):
        behind.append(hop(behind[-1], dz=1, mirror=True))
        if step < 4:
            front.append(hop(front[-1], dz=-1, mirror=True))
    return front + behind[:0:-1]


def pick_rows(column, mate, own_expert, row_count):
    blocks = jnp.concatenate([column, mate], axis=0)
    one_hot, weight = selection(blocks, own_expert)
    rows = jnp.einsum(
        "bjt,btd->bjd", one_hot, blocks[:, :row_count], preferred_element_type=F32
    ).astype(BF)
    return rows, one_hot, weight


def spread(one_hot, weight, out):
    dense = jnp.einsum("bjt,bjd->btd", one_hot, out, preferred_element_type=F32)
    return (dense * weight[:, :, None]).astype(BF)


def core_sum(dense):
    half = dense.shape[0] // 2
    return add(dense[:half], hop(dense[half:], swap=True))


def per_device(tokens, expert_ids, route_weights, expert_slot, w_gate, w_up, w_down):
    z = lax.axis_index("group")
    ep = lax.axis_index("ep")
    core = ep % 2
    row_count = tokens.shape[0]
    own_expert = jnp.sum(jnp.where(expert_slot == ep, jnp.arange(expert_slot.shape[0]), 0))
    start = jnp.where(core == 0, z, (N_Z - z) % N_Z)
    w_gate_up = jnp.concatenate([w_gate[0], w_up[0]], axis=1)
    down = w_down[0]
    block = pack(tokens, expert_ids, route_weights)
    from_behind = hop(block, dy=1, mirror=True)
    from_ahead = hop(block, dy=-1, mirror=True)
    from_below = hop(block, dx=1)
    from_above = hop(block, dx=-1)
    opposite = hop(block, dy=2, mirror=True)
    sides = jnp.stack([from_above, from_below])
    sides_behind = hop(sides, dy=1, mirror=True)
    sides_ahead = hop(sides, dy=-1, mirror=True)
    opposite_above = hop(opposite, dx=-1)
    opposite_below = hop(opposite, dx=1)
    column = jnp.stack([block, from_ahead, opposite, from_behind])
    mate = hop(column, swap=True)

    def prepared(column, mate):
        rows, one_hot, weight = pick_rows(column, mate, own_expert, row_count)
        rows = turn(rows, start)
        part = jnp.dot(
            rows.reshape(-1, rows.shape[-1]), w_gate_up, preferred_element_type=F32
        )
        part = part.astype(BF).reshape(rows.shape[:2] + (w_gate_up.shape[1],))
        return part, one_hot, weight

    def placed(hidden):
        out = jnp.zeros((N_Z,) + hidden[0].shape[:2] + (down.shape[1],), BF)
        for k in (0, 1, 7, 2, 6, 3, 5, 4):
            value = hidden[k]
            flat = value.reshape(-1, value.shape[-1])
            piece = jnp.dot(flat, down, preferred_element_type=F32).astype(BF)
            piece = piece.reshape((1,) + value.shape[:2] + (down.shape[1],))
            out = lax.dynamic_update_slice(out, piece, ((start + k) % N_Z, 0, 0, 0))
        return out

    def combined(first, second, out):
        dense = jnp.stack(
            [spread(first[1], first[2], out[:, 0]), spread(second[1], second[2], out[:, 1])],
            axis=1,
        )
        return core_sum(dense)

    chunk_0 = prepared(column, mate)
    above = jnp.stack([from_above, sides_ahead[0], opposite_above, sides_behind[0]])
    below = jnp.stack([from_below, sides_ahead[1], opposite_below, sides_behind[1]])
    far = hop(jnp.where(core == 0, below, above), dx=1, mirror=True)
    chunk_1 = prepared(above, hop(above, swap=True))
    hidden_0 = ring_sum(chunk_0[0])
    chunk_3 = prepared(below, hop(below, swap=True))
    hidden_1 = ring_sum(chunk_1[0])
    chunk_2 = prepared(far, hop(far, swap=True))
    hidden_3 = ring_sum(chunk_3[0])
    hidden_2 = ring_sum(chunk_2[0])
    gathered = ring_gather(jnp.stack([hidden_0, hidden_1]))
    kept_01 = combined(chunk_0, chunk_1, placed(gathered))
    out_3 = placed(ring_gather(hidden_3[None]))
    out_2 = placed(ring_gather(hidden_2[None]))
    kept_23 = combined(chunk_2, chunk_3, jnp.concatenate([out_2, out_3], axis=1))
    kept = jnp.concatenate([kept_01, kept_23], axis=1)
    kept = jnp.where(core == 0, kept, jnp.swapaxes(kept, 0, 1))
    partly = crossing_sum(kept, 0).astype(BF)
    return crossing_sum(partly, 1).astype(BF)


def solution(mesh):
    in_specs = (
        P("ep", "group"),
        P("ep", None),
        P("ep", None),
        P(),
        P("ep", "group", None),
        P("ep", "group", None),
        P("ep", None, "group"),
    )
    out_specs = P("ep", "group")
    return jax.shard_map(
        per_device, mesh=mesh, in_specs=in_specs, out_specs=out_specs, check_vma=False
    )
```

```python
import jax
import jax.numpy as jnp
from jax import lax
from jax.sharding import PartitionSpec as P

N_Z = 8
N_X = 4
N_Y = 4
CAP = 72
META_ROWS = 16
BF = jnp.bfloat16
F32 = jnp.float32


def hop(value, dz=0, dx=0, dy=0, mirror=False, swap=False):
    pairs = []
    for z in range(N_Z):
        for x in range(N_X):
            for y in range(N_Y):
                for c in range(2):
                    sign = -1 if (mirror and c) else 1
                    to_z = (z + sign * dz) % N_Z
                    to_x = (x + sign * dx) % N_X
                    to_y = (y + sign * dy) % N_Y
                    to_c = 1 - c if swap else c
                    here = ((z * N_X + x) * N_Y + y) * 2 + c
                    there = ((to_z * N_X + to_x) * N_Y + to_y) * 2 + to_c
                    pairs.append((here, there))
    return lax.ppermute(value, ("group", "ep"), pairs)


def crossing(value, step, stage):
    pairs = []
    for z in range(N_Z):
        for x in range(N_X):
            for y in range(N_Y):
                for c in range(2):
                    to_x, to_y = x, y
                    if stage == c:
                        to_y = (y + (1 - 2 * c) * step) % N_Y
                    else:
                        to_x = (x + step) % N_X
                    here = ((z * N_X + x) * N_Y + y) * 2 + c
                    there = ((z * N_X + to_x) * N_Y + to_y) * 2 + c
                    pairs.append((here, there))
    return lax.ppermute(value, ("group", "ep"), pairs)


def crossing_sum(groups, stage):
    to_next = crossing(groups[1], 1, stage)
    to_last = crossing(groups[3], -1, stage)
    across = crossing(groups[2], 2, stage)
    return (
        groups[0].astype(F32) + to_next.astype(F32)
        + to_last.astype(F32) + across.astype(F32)
    )


def add(first, second):
    return (first.astype(F32) + second.astype(F32)).astype(BF)


def pack(tokens, expert_ids, route_weights):
    high = route_weights.astype(BF)
    low = (route_weights - high.astype(F32)).astype(BF)
    ids = expert_ids.astype(BF)
    left = jnp.concatenate([ids.T, high.T], axis=0)
    right = jnp.concatenate([low.T, jnp.zeros_like(low.T)], axis=0)
    meta = jnp.concatenate([left, right], axis=1)
    meta = jnp.pad(meta, ((0, 0), (0, tokens.shape[1] - meta.shape[1])))
    return jnp.concatenate([tokens, meta], axis=0)


def selection(blocks, own_expert):
    rows = blocks.shape[1] - META_ROWS
    meta = blocks[:, rows:, :]
    ids = meta[:, 0:8, 0:rows]
    high = meta[:, 8:16, 0:rows].astype(F32)
    low = meta[:, 0:8, rows:2 * rows].astype(F32)
    hot = ids == own_expert.astype(BF)
    chosen = jnp.any(hot, axis=1)
    weight = jnp.sum(jnp.where(hot, high + low, 0.0), axis=1)
    order = jnp.arange(rows)
    before = (order[:, None] < order[None, :]).astype(BF)
    position = jnp.dot(chosen.astype(BF), before, preferred_element_type=F32).astype(jnp.int32)
    spot = jnp.where(chosen, position, -1)
    one_hot = (spot[:, None, :] == jnp.arange(CAP)[None, :, None]).astype(BF)
    return one_hot, weight


def turn(value, start):
    return lax.dynamic_slice_in_dim(jnp.concatenate([value, value], axis=0), start, N_Z, axis=0)


def ring_sum(part):
    ahead = hop(part[4], dz=1, mirror=True)
    back = hop(part[5], dz=-1, mirror=True)
    ahead = hop(add(ahead, part[3]), dz=1, mirror=True)
    back = hop(add(back, part[6]), dz=-1, mirror=True)
    ahead = hop(add(ahead, part[2]), dz=1, mirror=True)
    back = hop(add(back, part[7]), dz=-1, mirror=True)
    ahead = hop(add(ahead, part[1]), dz=1, mirror=True)
    total = part[0].astype(F32) + ahead.astype(F32) + back.astype(F32)
    hidden_width = part.shape[-1] // 2
    gate_sum, up_sum = total[:, :hidden_width], total[:, hidden_width:]
    return (jax.nn.silu(gate_sum) * up_sum).astype(BF)


def ring_gather(own):
    behind, front = [own], [own]
    for step in range(1, 5):
        behind.append(hop(behind[-1], dz=1, mirror=True))
        if step < 4:
            front.append(hop(front[-1], dz=-1, mirror=True))
    return front + behind[:0:-1]


def pick_rows(column, mate, own_expert, row_count):
    blocks = jnp.concatenate([column, mate], axis=0)
    one_hot, weight = selection(blocks, own_expert)
    rows = jnp.einsum(
        "bjt,btd->bjd", one_hot, blocks[:, :row_count], preferred_element_type=F32
    ).astype(BF)
    return rows, one_hot, weight


def spread(one_hot, weight, out):
    dense = jnp.einsum("bjt,bjd->btd", one_hot, out, preferred_element_type=F32)
    return (dense * weight[:, :, None]).astype(BF)


def core_sum(dense):
    half = dense.shape[0] // 2
    return add(dense[:half], hop(dense[half:], swap=True))


def per_device(tokens, expert_ids, route_weights, expert_slot, w_gate, w_up, w_down):
    z = lax.axis_index("group")
    ep = lax.axis_index("ep")
    core = ep % 2
    row_count = tokens.shape[0]
    own_expert = jnp.sum(jnp.where(expert_slot == ep, jnp.arange(expert_slot.shape[0]), 0))
    start = jnp.where(core == 0, z, (N_Z - z) % N_Z)
    w_gate_up = jnp.concatenate([w_gate[0], w_up[0]], axis=1)
    down = w_down[0]
    block = pack(tokens, expert_ids, route_weights)
    from_behind = hop(block, dy=1, mirror=True)
    from_ahead = hop(block, dy=-1, mirror=True)
    from_below = hop(block, dx=1)
    from_above = hop(block, dx=-1)
    opposite = hop(block, dy=2, mirror=True)
    sides = jnp.stack([from_above, from_below])
    sides_behind = hop(sides, dy=1, mirror=True)
    sides_ahead = hop(sides, dy=-1, mirror=True)
    opposite_above = hop(opposite, dx=-1)
    opposite_below = hop(opposite, dx=1)
    column = jnp.stack([block, from_ahead, opposite, from_behind])
    mate = hop(column, swap=True)

    def prepared(column, mate):
        rows, one_hot, weight = pick_rows(column, mate, own_expert, row_count)
        rows = turn(rows, start)
        part = jnp.dot(
            rows.reshape(-1, rows.shape[-1]), w_gate_up, preferred_element_type=F32
        )
        part = part.astype(BF).reshape(rows.shape[:2] + (w_gate_up.shape[1],))
        return part, one_hot, weight

    def placed(hidden):
        out = jnp.zeros((N_Z,) + hidden[0].shape[:2] + (down.shape[1],), BF)
        for k, value in enumerate(hidden):
            flat = value.reshape(-1, value.shape[-1])
            piece = jnp.dot(flat, down, preferred_element_type=F32).astype(BF)
            piece = piece.reshape((1,) + value.shape[:2] + (down.shape[1],))
            out = lax.dynamic_update_slice(out, piece, ((start + k) % N_Z, 0, 0, 0))
        return out

    def combined(first, second, out):
        dense = jnp.stack(
            [spread(first[1], first[2], out[:, 0]), spread(second[1], second[2], out[:, 1])],
            axis=1,
        )
        return core_sum(dense)

    chunk_0 = prepared(column, mate)
    above = jnp.stack([from_above, sides_ahead[0], opposite_above, sides_behind[0]])
    below = jnp.stack([from_below, sides_ahead[1], opposite_below, sides_behind[1]])
    far = hop(jnp.where(core == 0, below, above), dx=1, mirror=True)
    chunk_1 = prepared(above, hop(above, swap=True))
    hidden_0 = ring_sum(chunk_0[0])
    chunk_3 = prepared(below, hop(below, swap=True))
    hidden_1 = ring_sum(chunk_1[0])
    chunk_2 = prepared(far, hop(far, swap=True))
    hidden_3 = ring_sum(chunk_3[0])
    hidden_2 = ring_sum(chunk_2[0])
    gathered = ring_gather(jnp.stack([hidden_0, hidden_1]))
    kept_01 = combined(chunk_0, chunk_1, placed(gathered))
    out_3 = placed(ring_gather(hidden_3[None]))
    out_2 = placed(ring_gather(hidden_2[None]))
    kept_23 = combined(chunk_2, chunk_3, jnp.concatenate([out_2, out_3], axis=1))
    kept = jnp.concatenate([kept_01, kept_23], axis=1)
    kept = jnp.where(core == 0, kept, jnp.swapaxes(kept, 0, 1))
    partly = crossing_sum(kept, 0).astype(BF)
    return crossing_sum(partly, 1).astype(BF)


def solution(mesh):
    in_specs = (
        P("ep", "group"),
        P("ep", None),
        P("ep", None),
        P(),
        P("ep", "group", None),
        P("ep", "group", None),
        P("ep", None, "group"),
    )
    out_specs = P("ep", "group")
    return jax.shard_map(
        per_device, mesh=mesh, in_specs=in_specs, out_specs=out_specs, check_vma=False
    )
```
